32 devices in a mesh: space: 8 (over z, y), vel: 4 (over x, core).
Axes of the slice: x: 2, y: 2, z: 4, core: 2. Of those that a mesh axis runs over, the one named last changes fastest.
Arguments:
- start_right: float32 [4096, 2048], P('vel', 'space'), may hold values from -6 to 6
- start_left: float32 [4096, 2048], P('vel', 'space'), may hold values from -6 to 6
- collision: bfloat16 [4096, 4096], P('vel'), may hold values from -0.125 to 0.125
- frequency: float32 [2048], P('space'), may hold values from 0.5 to 4
- volume: float32 [2048], P('space'), may hold values from 0.25 to 1
- face_neighbor: int32 [6, 2048], P(None, 'space'), may hold values from 0 to 767, as said below
- face_area: float32 [6, 2048], P(None, 'space'), as said below
- send_slot: int32 [4, 1024], P(None, 'space'), may hold values from 0 to 255, as said below
Outputs:
- right_basis: float32 [5, 4096, 2048], P(None, 'vel', 'space')
- left_basis: float32 [5, 4096, 2048], P(None, 'vel', 'space')
- right_hess: float32 [5, 4], replicated
- left_hess: float32 [5, 4], replicated
- cross_gram: float32 [5, 5], replicated
The draws below stay inside these ranges and needn't reach their ends.
Inputs may be any that keep to these rules, and one draw needn't show every extreme that they name: `face_neighbor`: faces of a cell are ordered -x, +x, -y, +y, -z, +z. A value below 256 is a slot of the same block; a value 256 + g * 128 + k names entry k of what the block at offset (-2, 2, -1, 1)[g] provides in direction g. Every face of a cell and the face of the cell it reads form a mirrored pair. `face_area`: mirrored faces have equal areas; faces on the outer boundary of the domain have area 0, and so have faces across which face_neighbor points to no block. `send_slot`: entry (g, b * 128 + k) is a slot of block b: the cell that fills entry k of direction g for the block at offset -(-2, 2, -1, 1)[g] from b.
All inputs are finite; a program needn't handle non-finite values.
Results may differ from the reference program's by a relative error of at most 0.014.
Values may be sent and summed in bfloat16 or wider, within the bound.
A program may use at most 192 MiB of HBM per device.

```python
import math
import jax
import jax.numpy as jnp
from jax import lax

NV = 16
V = 4096
BSIDE = 2
GZ = 64
ITERS = 4
K = 256
FCAP = 128
BLOCKS = 8
NB = 2
GX = 8
GY = 4
NC = 2048


def block_layout(key):
    keys = jax.random.split(jax.random.fold_in(key, 11), BLOCKS)
    return jax.vmap(lambda one_key: jax.random.permutation(one_key, K))(keys).astype(jnp.int32)


def canonical_coords():
    canon = jnp.arange(K, dtype=jnp.int32)
    along_x = canon // (BSIDE * GZ)
    along_y = canon // GZ % BSIDE
    along_z = canon % GZ
    return (canon, along_x, along_y, along_z)


def place_cells(values, layout):
    target = jnp.arange(BLOCKS, dtype=jnp.int32)[:, None] * K + layout
    flat = jnp.zeros((values.shape[0], BLOCKS * K), values.dtype)
    return flat.at[:, target.reshape(-1)].set(values.reshape(values.shape[0], -1))


def draw_face_neighbor(key, part):
    layout = block_layout(key)
    canon, along_x, along_y, along_z = canonical_coords()

    def lookup(canon_ids):
        return jnp.take(layout, jnp.clip(canon_ids, 0, K - 1), axis=1)
    minus_x = jnp.where(along_x > 0, lookup(canon - BSIDE * GZ), K + along_y * GZ + along_z)
    plus_x = jnp.where(along_x < BSIDE - 1, lookup(canon + BSIDE * GZ), K + FCAP + along_y * GZ + along_z)
    minus_y = jnp.where(along_y > 0, lookup(canon - GZ), K + 2 * FCAP + along_x * GZ + along_z)
    plus_y = jnp.where(along_y < BSIDE - 1, lookup(canon + GZ), K + 3 * FCAP + along_x * GZ + along_z)
    minus_z = lookup(canon - along_z + (along_z - 1) % GZ)
    plus_z = lookup(canon - along_z + (along_z + 1) % GZ)
    stacked = jnp.stack([jnp.broadcast_to(item, (BLOCKS, K)) for item in (minus_x, plus_x, minus_y, plus_y, minus_z, plus_z)])
    return place_cells(stacked.astype(jnp.int32), layout)


def draw_send_slot(key, part):
    layout = block_layout(key)
    entry = jnp.arange(FCAP, dtype=jnp.int32)
    across = entry // GZ
    height = entry % GZ
    canon_lists = [((BSIDE - 1) * BSIDE + across) * GZ + height, across * GZ + height, (across * BSIDE + BSIDE - 1) * GZ + height, across * BSIDE * GZ + height]
    result = [jnp.take(layout, canon_ids, axis=1).reshape(-1) for canon_ids in canon_lists]
    return jnp.stack(result).astype(jnp.int32)


def draw_face_area(key, part):
    layout = block_layout(key)
    canon, along_x, along_y, along_z = canonical_coords()
    area_key = jax.random.fold_in(key, 23)
    key_x, key_y, key_z = jax.random.split(area_key, 3)
    lower, upper = (0.1, 1.0)
    faces_x = jax.random.uniform(key_x, (GX + 1, GY, GZ), jnp.float32, lower, upper)
    faces_y = jax.random.uniform(key_y, (GX, GY + 1, GZ), jnp.float32, lower, upper)
    faces_z = jax.random.uniform(key_z, (GX, GY, GZ), jnp.float32, lower, upper)
    index_x = jnp.arange(GX + 1)
    faces_x = faces_x * ((index_x > 0) & (index_x < GX)).astype(jnp.float32)[:, None, None]
    index_y = jnp.arange(GY + 1)
    faces_y = faces_y * ((index_y > 0) & (index_y < GY)).astype(jnp.float32)[None, :, None]
    block_ids = jnp.arange(BLOCKS, dtype=jnp.int32)[:, None]
    grid_x = block_ids // NB * BSIDE + along_x[None, :]
    grid_y = block_ids % NB * BSIDE + along_y[None, :]
    grid_z = jnp.broadcast_to(along_z[None, :], (BLOCKS, K))
    minus_x = faces_x[grid_x, grid_y, grid_z]
    plus_x = faces_x[grid_x + 1, grid_y, grid_z]
    minus_y = faces_y[grid_x, grid_y, grid_z]
    plus_y = faces_y[grid_x, grid_y + 1, grid_z]
    minus_z = faces_z[grid_x, grid_y, (grid_z - 1) % GZ]
    plus_z = faces_z[grid_x, grid_y, grid_z]
    stacked = jnp.stack([minus_x, plus_x, minus_y, plus_y, minus_z, plus_z])
    return place_cells(stacked, layout)


def raised(values, own_key, source, target, blocks, factor):
    owner, partner = [(jnp.arange(values.shape[dim]) // (values.shape[dim] // blocks)).reshape([-1 if axis == dim else 1 for axis in range(values.ndim)]) for dim in (source, target)]
    chosen = jax.random.permutation(own_key, blocks)[partner]
    strong = (owner == chosen) | (owner == (partner + blocks // 2) % blocks)
    return jnp.where(strong, factor * values, values)


def steps_of(own_key, extent, cuts, smallest, high):
    def one(dim, blocks):
        steps = jax.random.uniform(jax.random.fold_in(jax.random.fold_in(own_key, 6), dim), (blocks,), jnp.float32, smallest / len(cuts), high / len(cuts))
        return jnp.repeat(jnp.exp(steps), extent[dim] // blocks).reshape((-1,) + (1,) * (len(extent) - dim - 1))

    factor_of = one(*cuts[0])
    for cut in cuts[1:]:
        factor_of = factor_of * one(*cut)
    return factor_of


def noise(own_key, dims, deviation, limit, cuts=(), kind=jnp.bfloat16):
    values = jax.random.normal(own_key, dims, jnp.float32) * deviation
    if len(cuts) > 0:
        values = steps_of(own_key, dims, cuts, -0.22, 0.18) * values
    return jnp.clip(values, min=-limit, max=limit).astype(kind)


def gaussian_with(rng, shape, deviation, reach, cuts, heavy, held_as=jnp.bfloat16):
    values = deviation * jax.random.normal(rng, shape, jnp.float32)
    if cuts:
        values = values * steps_of(rng, shape, cuts, -0.22, 0.18)
    return jnp.clip(raised(values, jax.random.fold_in(rng, 3), *heavy), -reach, reach).astype(held_as)


def setup_inputs(seed: int = 0) -> dict:
    splits = jax.random.split(jax.random.key(seed), 9)
    return {
        "start_right": noise(splits[0], (V, NC), 1.0, 6.0, ((0, 4), (1, 8)), jnp.float32),
        "start_left": noise(splits[1], (V, NC), 1.0, 6.0, ((0, 4), (1, 8)), jnp.float32),
        "collision": gaussian_with(splits[2], (V, V), V ** -0.5, 0.125, ((0, 4),), (0, 1, 4, 2.0)),
        "frequency": jnp.clip(jnp.exp(math.log(4.0) - 2.0794415 * jax.random.uniform(splits[3], (NC,), jnp.float32) ** steps_of(splits[3], (NC,), ((0, 8),), -0.2, 0.2)), 0.5, 4.0),
        "volume": jnp.clip(jnp.exp(math.log(1.0) - 1.3862944 * jax.random.uniform(splits[4], (NC,), jnp.float32) ** steps_of(splits[4], (NC,), ((0, 8),), -0.2, 0.2)), 0.25, 1.0),
        "face_neighbor": draw_face_neighbor(jax.random.fold_in(splits[8], 71), 0),
        "face_area": draw_face_area(jax.random.fold_in(splits[8], 71), 0),
        "send_slot": draw_send_slot(jax.random.fold_in(splits[8], 71), 0),
    }


EPSILON = 1e-06

def face_speeds():
    velocity_ids = jnp.arange(V, dtype=jnp.int32)
    along_x = velocity_ids // (NV * NV)
    along_y = velocity_ids // NV % NV
    along_z = velocity_ids % NV
    centre = (NV - 1) / 2.0
    spacing = 6.0 / NV
    speed_x = (along_x.astype(jnp.float32) - centre) * spacing
    speed_y = (along_y.astype(jnp.float32) - centre) * spacing
    speed_z = (along_z.astype(jnp.float32) - centre) * spacing
    return [-speed_x, speed_x, -speed_y, speed_y, -speed_z, speed_z]

def neighbor_ids(face_neighbor, send_slot):
    cell_ids = jnp.arange(NC, dtype=jnp.int32)
    block_ids = cell_ids // K
    offsets = jnp.array([-NB, NB, -1, 1], dtype=jnp.int32)
    result = []
    for facing in range(6):
        slot_ids = face_neighbor[facing]
        local_ids = block_ids * K + jnp.minimum(slot_ids, K - 1)
        group_ids = jnp.clip((slot_ids - K) // FCAP, 0, 3)
        position = (slot_ids - K) % FCAP
        source_ids = jnp.clip(block_ids + offsets[group_ids], 0, BLOCKS - 1)
        remote_ids = source_ids * K + send_slot[group_ids, source_ids * FCAP + position]
        result.append(jnp.where(slot_ids < K, local_ids, remote_ids).astype(jnp.int32))
    return result

def transport(rounded, neighbors, face_area, inv_vol, speeds, adjoint):
    widened = rounded.astype(jnp.float32)
    running = jnp.zeros((V, NC), jnp.float32)
    for facing in range(6):
        speed_col = speeds[facing][:, None]
        beside = widened[:, neighbors[facing]]
        if adjoint:
            running = running + face_area[facing] * (jnp.maximum(speed_col, 0.0) * widened * inv_vol + jnp.minimum(-speed_col, 0.0) * beside * inv_vol[neighbors[facing]])
        else:
            running = running + face_area[facing] * inv_vol * (jnp.maximum(speed_col, 0.0) * widened + jnp.minimum(speed_col, 0.0) * beside)
    return running

def collide_forward(rounded, collision, frequency):
    return frequency[None, :] * jnp.dot(collision.T, rounded, preferred_element_type=jnp.float32)

def collide_adjoint(rounded, collision, frequency):
    return frequency[None, :] * jnp.dot(collision, rounded, preferred_element_type=jnp.float32)

def reference(start_right, start_left, collision, frequency, volume, face_neighbor, face_area, send_slot):
    speeds = face_speeds()
    neighbors = neighbor_ids(face_neighbor, send_slot)
    inv_vol = 1.0 / volume

    def operate(vector, adjoint):
        rounded = vector.astype(jnp.bfloat16)
        moved = transport(rounded, neighbors, face_area, inv_vol, speeds, adjoint)
        if adjoint:
            return moved + collide_adjoint(rounded, collision, frequency)
        return moved + collide_forward(rounded, collision, frequency)
    right_list = [start_right / jnp.sqrt(jnp.sum(start_right * start_right) + EPSILON)]
    left_list = [start_left / jnp.sqrt(jnp.sum(start_left * start_left) + EPSILON)]
    right_hess = jnp.zeros((ITERS + 1, ITERS), jnp.float32)
    left_hess = jnp.zeros((ITERS + 1, ITERS), jnp.float32)
    for column_idx in range(ITERS):
        right_new = operate(right_list[column_idx], False)
        left_new = operate(left_list[column_idx], True)
        right_coef = [jnp.sum(vector * right_new) for vector in right_list]
        left_coef = [jnp.sum(vector * left_new) for vector in left_list]
        for older in range(column_idx + 1):
            right_new = right_new - right_coef[older] * right_list[older]
            left_new = left_new - left_coef[older] * left_list[older]
            right_hess = right_hess.at[older, column_idx].set(right_coef[older])
            left_hess = left_hess.at[older, column_idx].set(left_coef[older])
        right_norm = jnp.sqrt(jnp.sum(right_new * right_new) + EPSILON)
        left_norm = jnp.sqrt(jnp.sum(left_new * left_new) + EPSILON)
        right_hess = right_hess.at[column_idx + 1, column_idx].set(right_norm)
        left_hess = left_hess.at[column_idx + 1, column_idx].set(left_norm)
        right_list.append(right_new / right_norm)
        left_list.append(left_new / left_norm)
    right_basis = jnp.stack(right_list)
    left_basis = jnp.stack(left_list)
    cross_gram = jnp.einsum('ivc,kvc->ik', left_basis, right_basis, precision=lax.Precision.HIGHEST)
    return (right_basis, left_basis, right_hess, left_hess, cross_gram)
```

```python
import functools

import jax
import jax.numpy as jnp
from jax import lax
from jax.experimental import pallas as pl
from jax.experimental.pallas import tpu as pltpu
from jax.sharding import PartitionSpec as P

NV = 16
ITERS = 4
EPSILON = 1e-06
LANES = 128
CHUNK = 256
MESH = pl.DeviceIdType.MESH
F32 = jnp.float32
BF16 = jnp.bfloat16


def dot(a, b):
    return jnp.dot(a, b, preferred_element_type=F32)


def kernel(
    sizes, start_r, start_l, coll_hbm, freq_ref, vol_ref, fn_ref, fa_ref, ss_ref,
    right_out, left_out, rh_out, lh_out, gram_out,
    coll, coll_t, pr, ql, wr, wl, hsend, halo, pack, gather, ivp, area_l,
    diag, speed, part, rs_send, rs_got, rs_xsend, rs_xgot,
    red_own, red_vel, red_mid, red_space,
    in_sem, out_sem, ag_send, ag_recv, rs_ssem, rs_rsem, h_send, h_recv,
    v_send, v_recv, s_send, s_recv,
):
    n_space, n_vel, row_blocks = sizes
    _, rows, cells = pr.shape
    face = hsend.shape[2]
    half = rows // 2
    steps = rows // CHUNK
    space = lax.axis_index("space")
    vel = lax.axis_index("vel")
    chip, core = vel // 2, vel % 2
    near = chip * 2 + (1 - core)
    far = (1 - chip) * 2 + core
    diagonal = (1 - chip) * 2 + (1 - core)
    offsets = [row_blocks, -row_blocks, 1, -1]

    def at(c):
        return pl.ds(pl.multiple_of(c * CHUNK, CHUNK), CHUNK)

    loads = [
        pltpu.make_async_copy(start_r, pr.at[0], in_sem.at[0]),
        pltpu.make_async_copy(start_l, ql.at[0], in_sem.at[1]),
        pltpu.make_async_copy(coll_hbm, coll, in_sem.at[2]),
    ]
    for load in loads:
        load.start()
    halo[...] = jnp.zeros_like(halo)

    barrier = pltpu.get_barrier_semaphore()
    for k in range(1, n_vel):
        pl.semaphore_signal(
            barrier, inc=1, device_id=(space, (vel + k) % n_vel), device_id_type=MESH
        )

    def greet(k, _):
        pl.semaphore_signal(
            barrier, inc=1, device_id=((space + k) % n_space, vel), device_id_type=MESH
        )
        return 0

    lax.fori_loop(1, n_space, greet, 0)
    pl.semaphore_wait(barrier, n_vel - 1 + n_space - 1)

    def send(src, dst, ssem, rsem, target):
        return pltpu.make_async_remote_copy(
            src_ref=src, dst_ref=dst, send_sem=ssem, recv_sem=rsem,
            device_id=target, device_id_type=MESH,
        )

    lane = lax.broadcasted_iota(jnp.int32, (8, LANES), 1)
    line = lax.broadcasted_iota(jnp.int32, (8, LANES), 0)

    def to_tile(accs):
        tile = jnp.zeros((8, LANES), F32)
        for k, acc in enumerate(accs):
            total = jnp.sum(jnp.sum(acc, axis=0, keepdims=True), axis=1, keepdims=True)
            tile = jnp.where((lane == k) & (line == 0), total, tile)
        return tile

    def all_sum(tile, turn):
        slot = turn % 2
        red_own[slot] = tile
        red_vel[slot, vel] = tile
        first = []
        for k in range(1, n_vel):
            copy = send(
                red_own.at[slot], red_vel.at[slot, vel], v_send.at[slot, k], v_recv.at[slot, vel],
                (space, (vel + k) % n_vel),
            )
            copy.start()
            first.append(copy)
        for k in range(1, n_vel):
            other = (vel + k) % n_vel
            send(
                red_own.at[slot], red_vel.at[slot, other], v_send.at[slot, k],
                v_recv.at[slot, other], (space, other),
            ).wait_recv()
        for copy in first:
            copy.wait_send()
        mid = red_vel[slot, 0]
        for k in range(1, n_vel):
            mid = mid + red_vel[slot, k]
        red_mid[slot] = mid
        red_space[slot, space] = mid

        def to(k):
            other = (space + k) % n_space
            return send(
                red_mid.at[slot], red_space.at[slot, space], s_send.at[slot, k],
                s_recv.at[slot, space], (other, vel),
            )

        def go(k, _):
            to(k).start()
            return 0

        def arrive(k, _):
            other = (space + k) % n_space
            send(
                red_mid.at[slot], red_space.at[slot, other], s_send.at[slot, k],
                s_recv.at[slot, other], (other, vel),
            ).wait_recv()
            return 0

        def left(k, _):
            to(k).wait_send()
            return 0

        lax.fori_loop(1, n_space, go, 0)
        lax.fori_loop(1, n_space, arrive, 0)
        lax.fori_loop(1, n_space, left, 0)
        total = red_space[slot, 0]
        for k in range(1, n_space):
            total = total + red_space[slot, k]
        return total

    def pick(tile, k):
        return tile[0:1, k : k + 1]

    def fold(x):
        return jnp.sum(x.reshape(CHUNK // 8, 8, cells), axis=0)

    zero = jnp.zeros((8, cells), F32)
    loads[0].wait()
    loads[1].wait()

    def squares(c, accs):
        r, l = pr[0, at(c), :], ql[0, at(c), :]
        return (accs[0] + fold(r * r), accs[1] + fold(l * l))

    lengths_tile = to_tile(lax.fori_loop(0, steps, squares, (zero, zero)))

    inv_vol = 1.0 / vol_ref[...]
    freq = freq_ref[...]
    sixteen = lax.broadcasted_iota(jnp.int32, (16, cells), 0)
    high = inv_vol.astype(BF16).astype(F32)
    middle = (inv_vol - high).astype(BF16).astype(F32)
    low = inv_vol - high - middle
    ivp[...] = jnp.where(
        sixteen == 0, high, jnp.where(sixteen == 1, middle, jnp.where(sixteen == 2, low, 0.0))
    ).astype(BF16)
    for f in range(6):
        depth = gather.shape[1]
        source = lax.broadcasted_iota(jnp.int32, (depth, cells), 0)
        gather[f] = jnp.where(source == fn_ref[f : f + 1, :], 1.0, 0.0).astype(BF16)
    source = lax.broadcasted_iota(jnp.int32, (cells, 4 * face), 0)
    pack[...] = jnp.where(source == ss_ref[...], 1.0, 0.0).astype(BF16)
    corner = dot(ivp[...], pack[...]).astype(BF16)
    for g in range(4):
        hsend[g, 2 * rows : 2 * rows + 16, :] = corner[:, g * face : (g + 1) * face]

    def prepare(c, _):
        ids = vel * rows + c * CHUNK + lax.broadcasted_iota(jnp.int32, (CHUNK, cells), 0)
        total = jnp.zeros((CHUNK, cells), F32)
        for axis, index in enumerate((ids // (NV * NV), ids // NV % NV, ids % NV)):
            xi = (index.astype(F32) - (NV - 1) / 2.0) * (6.0 / NV)
            speed[axis, at(c), :] = xi
            total = total + jnp.maximum(-xi, 0.0) * fa_ref[2 * axis : 2 * axis + 1, :]
            total = total + jnp.maximum(xi, 0.0) * fa_ref[2 * axis + 1 : 2 * axis + 2, :]
        diag[at(c), :] = total * inv_vol
        return 0

    lax.fori_loop(0, steps, prepare, 0)
    loads[2].wait()

    def turn_over(c, _):
        for r in range(steps):
            block = coll[r * CHUNK : (r + 1) * CHUNK, at(c)]
            coll_t[at(c), r * CHUNK : (r + 1) * CHUNK] = block.T
        return 0

    lax.fori_loop(0, coll.shape[1] // CHUNK, turn_over, 0)
    lengths = all_sum(lengths_tile, 0)
    inv_r = 1.0 / jnp.sqrt(pick(lengths, 0) + EPSILON)
    inv_l = 1.0 / jnp.sqrt(pick(lengths, 1) + EPSILON)

    def scale(c, _):
        r, l = pr[0, at(c), :] * inv_r, ql[0, at(c), :] * inv_l
        pr[0, at(c), :] = r
        ql[0, at(c), :] = l
        wr[at(c), :] = r.astype(BF16)
        wl[0, at(c), :] = l.astype(BF16)
        return 0

    lax.fori_loop(0, steps, scale, 0)

    def leave(j):
        copies = [
            pltpu.make_async_copy(pr.at[j], right_out.at[j], out_sem.at[0, j]),
            pltpu.make_async_copy(ql.at[j], left_out.at[j], out_sem.at[1, j]),
        ]
        for copy in copies:
            copy.start()
        return copies

    outgoing = leave(0)
    gram = jnp.zeros((8, LANES), F32)
    right_hess = jnp.zeros((8, LANES), F32)
    left_hess = jnp.zeros((8, LANES), F32)

    def pairs(j):
        return [(j, k) for k in range(j + 1)] + [(i, j) for i in range(j)]

    def add_gram(gram, accs, j):
        for (i, k), acc in zip(pairs(j), accs):
            total = jnp.sum(jnp.sum(acc, axis=0, keepdims=True), axis=1, keepdims=True)
            place = i * (ITERS + 1) + k
            gram = jnp.where((lane == place) & (line == 0), total, gram)
        return gram

    def partial_sums(owner, c):
        start = pl.multiple_of(owner * rows + c * CHUNK, CHUNK)
        return dot(coll_t[pl.ds(start, CHUNK), :], wr[...])

    def adjoint_part(owner, slot, c):
        columns = pl.ds(pl.multiple_of(owner * rows, rows), rows)
        return dot(coll[at(c), columns], wl[slot])

    def halo_sends(started):
        for g in range(4):
            to, source = space + offsets[g], space - offsets[g]
            copy = send(
                hsend.at[g], halo.at[g], h_send.at[g], h_recv.at[g],
                ((to + n_space) % n_space, vel),
            )
            if started == "start":
                pl.when((to >= 0) & (to < n_space))(copy.start)
            elif started == "sent":
                pl.when((to >= 0) & (to < n_space))(copy.wait_send)
            else:
                pl.when((source >= 0) & (source < n_space))(copy.wait_recv)

    for j in range(ITERS):
        parts = [pl.ds(0, half), pl.ds(half, half)]
        across = [
            send(wl.at[0, p], wl.at[2, p], ag_send.at[h], ag_recv.at[h], (space, far))
            for h, p in enumerate(parts)
        ]
        beside = send(wl.at[0], wl.at[1], ag_send.at[2], ag_recv.at[2], (space, near))
        for copy in across:
            copy.start()
        beside.start()

        summed = []
        for slot, owner in ((1, diagonal), (0, near)):
            def product(c, _, slot=slot, owner=owner):
                rs_send[slot, at(c), :] = partial_sums(owner, c).astype(BF16)
                return 0

            lax.fori_loop(0, steps, product, 0)
            copy = send(
                rs_send.at[slot], rs_got.at[slot], rs_ssem.at[slot], rs_rsem.at[slot],
                (space, near),
            )
            copy.start()
            summed.append(copy)

        def packing(c, _):
            for t in range(2):
                vector = wr[at(c), :] if t == 0 else wl[0, at(c), :]
                out = dot(vector, pack[...]).astype(BF16)
                where = pl.ds(pl.multiple_of(t * rows + c * CHUNK, CHUNK), CHUNK)
                for g in range(4):
                    hsend[g, where, :] = out[:, g * face : (g + 1) * face]
            return 0

        lax.fori_loop(0, steps, packing, 0)
        halo_sends("start")

        def far_part(c, _):
            part[at(c), :] = partial_sums(far, c)
            return 0

        lax.fori_loop(0, steps, far_part, 0)
        summed[0].wait_recv()
        shipped = []
        for h, p in enumerate(parts):
            def joined(c, _):
                rs_xsend[at(c), :] = (part[at(c), :] + rs_got[1, at(c), :].astype(F32)).astype(BF16)
                return 0

            lax.fori_loop(h * (steps // 2), (h + 1) * (steps // 2), joined, 0)
            copy = send(
                rs_xsend.at[p], rs_xgot.at[p], rs_ssem.at[2 + h], rs_rsem.at[2 + h], (space, far)
            )
            copy.start()
            shipped.append(copy)

        def own_part(c, _):
            pr[j + 1, at(c), :] = partial_sums(vel, c)
            ql[j + 1, at(c), :] = adjoint_part(vel, 0, c)
            return 0

        lax.fori_loop(0, steps, own_part, 0)
        beside.wait_recv()
        summed[1].wait_recv()

        def near_part(c, _):
            pr[j + 1, at(c), :] = freq * (pr[j + 1, at(c), :] + rs_got[0, at(c), :].astype(F32))
            ql[j + 1, at(c), :] = ql[j + 1, at(c), :] + adjoint_part(near, 1, c)
            return 0

        lax.fori_loop(0, steps, near_part, 0)
        passed = []
        for h, p in enumerate(parts):
            across[h].wait_recv()
            copy = send(
                wl.at[2, p], wl.at[3, p], ag_send.at[3 + h], ag_recv.at[3 + h], (space, near)
            )
            copy.start()
            passed.append(copy)

        halo_sends("arrive")
        if j == 0:
            for f in range(6):
                known = jnp.concatenate(
                    [ivp[...]] + [halo[g, 2 * rows : 2 * rows + 16, :] for g in range(4)], axis=1
                )
                three = dot(known, gather[f])
                area_l[f : f + 1, :] = fa_ref[f : f + 1, :] * jnp.sum(
                    three, axis=0, keepdims=True
                )

        def transport(c, _):
            for t, basis in ((0, pr), (1, ql)):
                vector = wr[at(c), :] if t == 0 else wl[0, at(c), :]
                where = pl.ds(pl.multiple_of(t * rows + c * CHUNK, CHUNK), CHUNK)
                extended = jnp.concatenate(
                    [vector] + [halo[g, where, :] for g in range(4)], axis=1
                )
                out = diag[at(c), :] * vector.astype(F32)
                for f in range(6):
                    xi = speed[f // 2, at(c), :]
                    inward = xi if (f + t) % 2 == 1 else -xi
                    if t == 0:
                        weight = fa_ref[f : f + 1, :] * inv_vol
                    else:
                        weight = area_l[f : f + 1, :]
                    out = out + jnp.minimum(inward, 0.0) * (weight * dot(extended, gather[f]))
                if t == 0:
                    basis[j + 1, at(c), :] = basis[j + 1, at(c), :] + out
                else:
                    part[at(c), :] = out
            return 0

        lax.fori_loop(0, steps, transport, 0)

        def gram_step(c, accs):
            return tuple(
                acc + fold(ql[i, at(c), :] * pr[k, at(c), :])
                for (i, k), acc in zip(pairs(j), accs)
            )

        accs = lax.fori_loop(0, steps, gram_step, (zero,) * len(pairs(j)))
        gram = add_gram(gram, accs, j)

        for copy in passed:
            copy.wait_recv()

        def left_end(c, accs):
            total = ql[j + 1, at(c), :] + adjoint_part(far, 2, c) + adjoint_part(diagonal, 3, c)
            new = part[at(c), :] + freq * total
            ql[j + 1, at(c), :] = new
            return tuple(
                acc + fold(new * (ql[i, at(c), :] if i <= j else new))
                for i, acc in enumerate(accs)
            )

        left_dots = lax.fori_loop(0, steps, left_end, (zero,) * (j + 2))

        def right_end(c, accs):
            new = pr[j + 1, at(c), :] + freq * rs_xgot[at(c), :].astype(F32)
            pr[j + 1, at(c), :] = new
            return tuple(
                acc + fold(new * (pr[i, at(c), :] if i <= j else new))
                for i, acc in enumerate(accs)
            )

        right_dots = (zero,) * (j + 2)
        for h in range(2):
            shipped[h].wait_recv()
            right_dots = lax.fori_loop(
                h * (steps // 2), (h + 1) * (steps // 2), right_end, right_dots
            )
        for copy in across + [beside] + summed + shipped + passed:
            copy.wait_send()
        halo_sends("sent")

        sums = all_sum(to_tile(list(right_dots) + list(left_dots)), j + 1)
        right_coef = [pick(sums, i) for i in range(j + 1)]
        left_coef = [pick(sums, j + 2 + i) for i in range(j + 1)]
        right_raw, left_raw = pick(sums, j + 1), pick(sums, 2 * j + 3)
        for i in range(j + 1):
            right_raw = right_raw - right_coef[i] * right_coef[i]
            left_raw = left_raw - left_coef[i] * left_coef[i]
        right_norm = jnp.sqrt(right_raw + EPSILON)
        left_norm = jnp.sqrt(left_raw + EPSILON)
        for i in range(j + 2):
            here = (line == i) & (lane == j)
            right_hess = jnp.where(here, right_coef[i] if i <= j else right_norm, right_hess)
            left_hess = jnp.where(here, left_coef[i] if i <= j else left_norm, left_hess)
        inv_r, inv_l = 1.0 / right_norm, 1.0 / left_norm
        last = j == ITERS - 1

        def finish(c, accs):
            r, l = pr[j + 1, at(c), :], ql[j + 1, at(c), :]
            for i in range(j + 1):
                r = r - right_coef[i] * pr[i, at(c), :]
                l = l - left_coef[i] * ql[i, at(c), :]
            r, l = r * inv_r, l * inv_l
            pr[j + 1, at(c), :] = r
            ql[j + 1, at(c), :] = l
            if not last:
                wr[at(c), :] = r.astype(BF16)
                wl[0, at(c), :] = l.astype(BF16)
            return accs

        lax.fori_loop(0, steps, finish, 0)
        outgoing += leave(j + 1)

    def gram_last(c, accs):
        return tuple(
            acc + fold(ql[i, at(c), :] * pr[k, at(c), :])
            for (i, k), acc in zip(pairs(ITERS), accs)
        )

    accs = lax.fori_loop(0, steps, gram_last, (zero,) * len(pairs(ITERS)))
    total = all_sum(add_gram(gram, accs, ITERS), ITERS + 1)
    gram_tile = jnp.zeros((8, LANES), F32)
    for i in range(ITERS + 1):
        for k in range(ITERS + 1):
            gram_tile = jnp.where(
                (line == i) & (lane == k), pick(total, i * (ITERS + 1) + k), gram_tile
            )
    gram_out[...] = gram_tile[: ITERS + 1, : ITERS + 1]
    rh_out[...] = right_hess[: ITERS + 1, :ITERS]
    lh_out[...] = left_hess[: ITERS + 1, :ITERS]
    for copy in outgoing:
        copy.wait()


def per_device(
    start_right, start_left, collision, frequency, volume, face_neighbor, face_area, send_slot
):
    rows, cells = start_right.shape
    face = send_slot.shape[1]
    n_space, n_vel = lax.axis_size("space"), lax.axis_size("vel")
    assert n_vel == 4 and rows % (2 * CHUNK) == 0
    depth = cells + 4 * face
    tall = 2 * rows + 16
    vmem = pl.BlockSpec(memory_space=pltpu.VMEM)
    hbm = pl.BlockSpec(memory_space=pl.ANY)
    basis = jax.ShapeDtypeStruct((ITERS + 1, rows, cells), F32)
    hess = jax.ShapeDtypeStruct((ITERS + 1, ITERS), F32)
    dma = pltpu.SemaphoreType.DMA
    return pl.pallas_call(
        functools.partial(kernel, (n_space, n_vel, n_space // 4)),
        out_shape=(
            basis, basis, hess, hess, jax.ShapeDtypeStruct((ITERS + 1, ITERS + 1), F32)
        ),
        in_specs=[hbm] * 3 + [vmem] * 5,
        out_specs=(hbm, hbm, vmem, vmem, vmem),
        scratch_shapes=[
            pltpu.VMEM(collision.shape, BF16),
            pltpu.VMEM((collision.shape[1], rows), BF16),
            pltpu.VMEM((ITERS + 1, rows, cells), F32),
            pltpu.VMEM((ITERS + 1, rows, cells), F32),
            pltpu.VMEM((rows, cells), BF16),
            pltpu.VMEM((4, rows, cells), BF16),
            pltpu.VMEM((4, tall, face), BF16),
            pltpu.VMEM((4, tall, face), BF16),
            pltpu.VMEM((cells, 4 * face), BF16),
            pltpu.VMEM((6, depth, cells), BF16),
            pltpu.VMEM((16, cells), BF16),
            pltpu.VMEM((8, cells), F32),
            pltpu.VMEM((rows, cells), F32),
            pltpu.VMEM((3, rows, cells), F32),
            pltpu.VMEM((rows, cells), F32),
            pltpu.VMEM((2, rows, cells), BF16),
            pltpu.VMEM((2, rows, cells), BF16),
            pltpu.VMEM((rows, cells), BF16),
            pltpu.VMEM((rows, cells), BF16),
            pltpu.VMEM((2, 8, LANES), F32),
            pltpu.VMEM((2, n_vel, 8, LANES), F32),
            pltpu.VMEM((2, 8, LANES), F32),
            pltpu.VMEM((2, n_space, 8, LANES), F32),
            dma((3,)),
            dma((2, ITERS + 1)),
            dma((5,)),
            dma((5,)),
            dma((4,)),
            dma((4,)),
            dma((4,)),
            dma((4,)),
            dma((2, n_vel)),
            dma((2, n_vel)),
            dma((2, n_space)),
            dma((2, n_space)),
        ],
        compiler_params=pltpu.CompilerParams(
            collective_id=0, has_side_effects=True, vmem_limit_bytes=60 * 1024 * 1024
        ),
    )(
        start_right, start_left, collision, frequency.reshape(1, -1), volume.reshape(1, -1),
        face_neighbor, face_area, send_slot.reshape(1, -1),
    )


def solution(mesh):
    placed = (
        P("vel", "space"),
        P("vel", "space"),
        P("vel", None),
        P("space"),
        P("space"),
        P(None, "space"),
        P(None, "space"),
        P(None, "space"),
    )
    return jax.shard_map(
        per_device,
        mesh=mesh,
        in_specs=placed,
        out_specs=(P(None, "vel", "space"), P(None, "vel", "space"), P(), P(), P()),
        check_vma=False,
    )
```

```python
import functools

import jax
import jax.numpy as jnp
from jax import lax
from jax.experimental import pallas as pl
from jax.experimental.pallas import tpu as pltpu
from jax.sharding import PartitionSpec as P

NV = 16
ITERS = 4
EPSILON = 1e-06
LANES = 128
CHUNK = NV * NV
MESH = pl.DeviceIdType.MESH
F32 = jnp.float32
BF16 = jnp.bfloat16


def dot(a, b):
    return jnp.dot(a, b, preferred_element_type=F32)


def kernel(
    sizes, start_r, start_l, coll_hbm, freq_ref, vol_ref, fn_ref, fa_ref, ss_ref,
    right_out, left_out, rh_out, lh_out, gram_out,
    coll, coll_t, pr, ql, wr, wl, hsend, halo, pack, gather, ivp, area_l,
    diag, coef, part, rs_send, rs_got, rs_xsend, rs_xgot,
    red_own, red_vel, red_mid, red_space,
    in_sem, out_sem, ag_send, ag_recv, rs_ssem, rs_rsem, h_send, h_recv,
    v_send, v_recv, s_send, s_recv,
):
    n_space, n_vel, row_blocks = sizes
    _, rows, cells = pr.shape
    face = hsend.shape[2]
    half = rows // 2
    steps = rows // CHUNK
    space = lax.axis_index("space")
    vel = lax.axis_index("vel")
    chip, core = vel // 2, vel % 2
    near = chip * 2 + (1 - core)
    far = (1 - chip) * 2 + core
    diagonal = (1 - chip) * 2 + (1 - core)
    offsets = [row_blocks, -row_blocks, 1, -1]

    def at(c):
        return pl.ds(pl.multiple_of(c * CHUNK, CHUNK), CHUNK)

    loads = [
        pltpu.make_async_copy(start_r, pr.at[0], in_sem.at[0]),
        pltpu.make_async_copy(start_l, ql.at[0], in_sem.at[1]),
        pltpu.make_async_copy(coll_hbm, coll, in_sem.at[2]),
    ]
    for load in loads:
        load.start()
    halo[...] = jnp.zeros_like(halo)

    barrier = pltpu.get_barrier_semaphore()
    for k in range(1, n_vel):
        pl.semaphore_signal(
            barrier, inc=1, device_id=(space, (vel + k) % n_vel), device_id_type=MESH
        )

    def greet(k, _):
        pl.semaphore_signal(
            barrier, inc=1, device_id=((space + k) % n_space, vel), device_id_type=MESH
        )
        return 0

    lax.fori_loop(1, n_space, greet, 0)
    pl.semaphore_wait(barrier, n_vel - 1 + n_space - 1)

    def send(src, dst, ssem, rsem, target):
        return pltpu.make_async_remote_copy(
            src_ref=src, dst_ref=dst, send_sem=ssem, recv_sem=rsem,
            device_id=target, device_id_type=MESH,
        )

    lane = lax.broadcasted_iota(jnp.int32, (8, LANES), 1)
    line = lax.broadcasted_iota(jnp.int32, (8, LANES), 0)

    def to_tile(accs):
        tile = jnp.zeros((8, LANES), F32)
        for k, acc in enumerate(accs):
            total = jnp.sum(jnp.sum(acc, axis=0, keepdims=True), axis=1, keepdims=True)
            tile = jnp.where((lane == k) & (line == 0), total, tile)
        return tile

    def all_sum(tile, turn):
        slot = turn % 2
        red_own[slot] = tile
        red_vel[slot, vel] = tile
        first = []
        for k in range(1, n_vel):
            copy = send(
                red_own.at[slot], red_vel.at[slot, vel], v_send.at[slot, k], v_recv.at[slot, vel],
                (space, (vel + k) % n_vel),
            )
            copy.start()
            first.append(copy)
        for k in range(1, n_vel):
            other = (vel + k) % n_vel
            send(
                red_own.at[slot], red_vel.at[slot, other], v_send.at[slot, k],
                v_recv.at[slot, other], (space, other),
            ).wait_recv()
        mid = red_vel[slot, 0]
        for k in range(1, n_vel):
            mid = mid + red_vel[slot, k]
        red_mid[slot] = mid
        red_space[slot, space] = mid

        def to(k):
            other = (space + k) % n_space
            return send(
                red_mid.at[slot], red_space.at[slot, space], s_send.at[slot, k],
                s_recv.at[slot, space], (other, vel),
            )

        def go(k, _):
            to(k).start()
            return 0

        def arrive(k, _):
            other = (space + k) % n_space
            send(
                red_mid.at[slot], red_space.at[slot, other], s_send.at[slot, k],
                s_recv.at[slot, other], (other, vel),
            ).wait_recv()
            return 0

        def left(k, _):
            to(k).wait_send()
            return 0

        lax.fori_loop(1, n_space, go, 0)
        lax.fori_loop(1, n_space, arrive, 0)
        for copy in first:
            copy.wait_send()
        lax.fori_loop(1, n_space, left, 0)
        total = red_space[slot, 0]
        for k in range(1, n_space):
            total = total + red_space[slot, k]
        return total

    def pick(tile, k):
        return tile[0:1, k : k + 1]

    def fold(x):
        return jnp.sum(x.reshape(CHUNK // 8, 8, cells), axis=0)

    zero = jnp.zeros((8, cells), F32)
    loads[0].wait()
    loads[1].wait()

    def squares(c, accs):
        r, l = pr[0, at(c), :], ql[0, at(c), :]
        return (accs[0] + fold(r * r), accs[1] + fold(l * l))

    lengths_tile = to_tile(lax.fori_loop(0, steps, squares, (zero, zero)))

    inv_vol = 1.0 / vol_ref[...]
    freq = freq_ref[...]
    sixteen = lax.broadcasted_iota(jnp.int32, (16, cells), 0)
    high = inv_vol.astype(BF16).astype(F32)
    middle = (inv_vol - high).astype(BF16).astype(F32)
    low = inv_vol - high - middle
    ivp[...] = jnp.where(
        sixteen == 0, high, jnp.where(sixteen == 1, middle, jnp.where(sixteen == 2, low, 0.0))
    ).astype(BF16)
    for f in range(6):
        source = lax.broadcasted_iota(jnp.int32, (gather.shape[0], cells), 0)
        gather[:, f * cells : (f + 1) * cells] = jnp.where(
            source == fn_ref[f : f + 1, :], 1.0, 0.0
        ).astype(BF16)
    source = lax.broadcasted_iota(jnp.int32, (cells, 4 * face), 0)
    pack[...] = jnp.where(source == ss_ref[...], 1.0, 0.0).astype(BF16)
    corner = dot(ivp[...], pack[...]).astype(BF16)
    for g in range(4):
        hsend[g, 2 * rows : 2 * rows + 16, :] = corner[:, g * face : (g + 1) * face]

    def prepare(c, _):
        ids = vel * rows + c * CHUNK + lax.broadcasted_iota(jnp.int32, (CHUNK, cells), 0)
        total = jnp.zeros((CHUNK, cells), F32)
        for axis, index in enumerate((ids // (NV * NV), ids // NV % NV, ids % NV)):
            xi = (index.astype(F32) - (NV - 1) / 2.0) * (6.0 / NV)
            total = total + jnp.maximum(-xi, 0.0) * fa_ref[2 * axis : 2 * axis + 1, :]
            total = total + jnp.maximum(xi, 0.0) * fa_ref[2 * axis + 1 : 2 * axis + 2, :]
        diag[at(c), :] = total * inv_vol
        return 0

    lax.fori_loop(0, steps, prepare, 0)
    loads[2].wait()

    def turn_over(c, _):
        for r in range(steps):
            block = coll[r * CHUNK : (r + 1) * CHUNK, at(c)]
            coll_t[at(c), r * CHUNK : (r + 1) * CHUNK] = block.T
        return 0

    lax.fori_loop(0, coll.shape[1] // CHUNK, turn_over, 0)
    lengths = all_sum(lengths_tile, 0)
    inv_r = 1.0 / jnp.sqrt(pick(lengths, 0) + EPSILON)
    inv_l = 1.0 / jnp.sqrt(pick(lengths, 1) + EPSILON)

    def scale(c, _):
        r, l = pr[0, at(c), :] * inv_r, ql[0, at(c), :] * inv_l
        pr[0, at(c), :] = r
        ql[0, at(c), :] = l
        wr[at(c), :] = r.astype(BF16)
        wl[0, at(c), :] = l.astype(BF16)
        return 0

    lax.fori_loop(0, steps, scale, 0)

    def leave(j):
        copies = [
            pltpu.make_async_copy(pr.at[j], right_out.at[j], out_sem.at[0, j]),
            pltpu.make_async_copy(ql.at[j], left_out.at[j], out_sem.at[1, j]),
        ]
        for copy in copies:
            copy.start()
        return copies

    outgoing = leave(0)
    gram = jnp.zeros((8, LANES), F32)
    right_hess = jnp.zeros((8, LANES), F32)
    left_hess = jnp.zeros((8, LANES), F32)

    def pairs(j):
        return [(j, k) for k in range(j + 1)] + [(i, j) for i in range(j)]

    def add_gram(gram, accs, j):
        for (i, k), acc in zip(pairs(j), accs):
            total = jnp.sum(jnp.sum(acc, axis=0, keepdims=True), axis=1, keepdims=True)
            place = i * (ITERS + 1) + k
            gram = jnp.where((lane == place) & (line == 0), total, gram)
        return gram

    def partial_sums(owner, c):
        start = pl.multiple_of(owner * rows + c * CHUNK, CHUNK)
        return dot(coll_t[pl.ds(start, CHUNK), :], wr[...])

    def adjoint_part(owner, slot, c):
        columns = pl.ds(pl.multiple_of(owner * rows, rows), rows)
        return dot(coll[at(c), columns], wl[slot])

    def halo_sends(started):
        for g in range(4):
            to = space + offsets[g]
            place, extent = (space, n_space) if g < 2 else (space % row_blocks, row_blocks)
            goes = (place + offsets[g] >= 0) & (place + offsets[g] < extent)
            comes = (place - offsets[g] >= 0) & (place - offsets[g] < extent)
            copy = send(
                hsend.at[g], halo.at[g], h_send.at[g], h_recv.at[g],
                ((to + n_space) % n_space, vel),
            )
            if started == "start":
                pl.when(goes)(copy.start)
            elif started == "sent":
                pl.when(goes)(copy.wait_send)
            else:
                pl.when(comes)(copy.wait_recv)

    for j in range(ITERS):
        parts = [pl.ds(0, half), pl.ds(half, half)]
        across = [
            send(wl.at[0, p], wl.at[2, p], ag_send.at[h], ag_recv.at[h], (space, far))
            for h, p in enumerate(parts)
        ]
        beside = send(wl.at[0], wl.at[1], ag_send.at[2], ag_recv.at[2], (space, near))
        for copy in across:
            copy.start()
        beside.start()

        summed = []
        for slot, owner in ((1, diagonal), (0, near)):
            def product(c, _, slot=slot, owner=owner):
                rs_send[slot, at(c), :] = partial_sums(owner, c).astype(BF16)
                return 0

            lax.fori_loop(0, steps, product, 0)
            copy = send(
                rs_send.at[slot], rs_got.at[slot], rs_ssem.at[slot], rs_rsem.at[slot],
                (space, near),
            )
            copy.start()
            summed.append(copy)

        def packing(c, _):
            for t in range(2):
                vector = wr[at(c), :] if t == 0 else wl[0, at(c), :]
                out = dot(vector, pack[...]).astype(BF16)
                where = pl.ds(pl.multiple_of(t * rows + c * CHUNK, CHUNK), CHUNK)
                for g in range(4):
                    hsend[g, where, :] = out[:, g * face : (g + 1) * face]
            return 0

        lax.fori_loop(0, steps, packing, 0)
        halo_sends("start")

        def far_part(c, _):
            part[at(c), :] = partial_sums(far, c)
            return 0

        lax.fori_loop(0, steps, far_part, 0)
        summed[0].wait_recv()
        shipped = []
        for h, p in enumerate(parts):
            def joined(c, _):
                rs_xsend[at(c), :] = (part[at(c), :] + rs_got[1, at(c), :].astype(F32)).astype(BF16)
                return 0

            lax.fori_loop(h * (steps // 2), (h + 1) * (steps // 2), joined, 0)
            copy = send(
                rs_xsend.at[p], rs_xgot.at[p], rs_ssem.at[2 + h], rs_rsem.at[2 + h], (space, far)
            )
            copy.start()
            shipped.append(copy)

        def own_part(c, _):
            pr[j + 1, at(c), :] = partial_sums(vel, c)
            ql[j + 1, at(c), :] = adjoint_part(vel, 0, c)
            return 0

        lax.fori_loop(0, steps, own_part, 0)
        beside.wait_recv()
        summed[1].wait_recv()

        def near_part(c, _):
            pr[j + 1, at(c), :] = freq * (pr[j + 1, at(c), :] + rs_got[0, at(c), :].astype(F32))
            ql[j + 1, at(c), :] = ql[j + 1, at(c), :] + adjoint_part(near, 1, c)
            return 0

        lax.fori_loop(0, steps, near_part, 0)
        passed = []
        for h, p in enumerate(parts):
            across[h].wait_recv()
            copy = send(
                wl.at[2, p], wl.at[3, p], ag_send.at[3 + h], ag_recv.at[3 + h], (space, near)
            )
            copy.start()
            passed.append(copy)

        halo_sends("arrive")
        if j == 0:
            for f in range(6):
                known = jnp.concatenate(
                    [ivp[...]] + [halo[g, 2 * rows : 2 * rows + 16, :] for g in range(4)], axis=1
                )
                three = dot(known, gather[:, f * cells : (f + 1) * cells])
                area_l[f : f + 1, :] = fa_ref[f : f + 1, :] * jnp.sum(
                    three, axis=0, keepdims=True
                )

            def weights(c, _):
                ids = vel * rows + c * CHUNK + lax.broadcasted_iota(jnp.int32, (CHUNK, cells), 0)
                for axis, index in enumerate((ids // (NV * NV), ids // NV % NV, ids % NV)):
                    xi = (index.astype(F32) - (NV - 1) / 2.0) * (6.0 / NV)
                    low, high = slice(2 * axis, 2 * axis + 1), slice(2 * axis + 1, 2 * axis + 2)
                    coef[0, axis, at(c), :] = inv_vol * (
                        jnp.minimum(-xi, 0.0) * fa_ref[low, :]
                        + jnp.minimum(xi, 0.0) * fa_ref[high, :]
                    )
                    coef[1, axis, at(c), :] = (
                        jnp.minimum(xi, 0.0) * area_l[low, :]
                        + jnp.minimum(-xi, 0.0) * area_l[high, :]
                    )
                return 0

            lax.fori_loop(0, steps, weights, 0)

        def transport(c, _):
            for t, basis in ((0, pr), (1, ql)):
                vector = wr[at(c), :] if t == 0 else wl[0, at(c), :]
                where = pl.ds(pl.multiple_of(t * rows + c * CHUNK, CHUNK), CHUNK)
                extended = jnp.concatenate(
                    [vector] + [halo[g, where, :] for g in range(4)], axis=1
                )
                plane = (vel * rows + c * CHUNK) // (NV * NV)
                side = (plane // (NV // 2) + 1 + t) % 2
                along_x = pl.ds(pl.multiple_of(side * cells, cells), cells)
                got_x = dot(extended, gather[:, along_x])
                first = 3 if t == 0 else 2
                got_y = jnp.concatenate(
                    [
                        dot(extended[: CHUNK // 2], gather[:, first * cells : (first + 1) * cells]),
                        dot(extended[CHUNK // 2 :], gather[:, (5 - first) * cells : (6 - first) * cells]),
                    ],
                    axis=0,
                )
                both = dot(extended, gather[:, 4 * cells :])
                tiles = both.reshape(CHUNK // NV, 2, NV // 2, 2 * cells)
                one, two = tiles[:, 0], tiles[:, 1]
                below, above = (one[..., cells:], two[..., :cells])
                if t == 1:
                    below, above = (one[..., :cells], two[..., cells:])
                got_z = jnp.stack([below, above], axis=1).reshape(CHUNK, cells)
                out = diag[at(c), :] * vector.astype(F32)
                out = out + coef[t, 0, at(c), :] * got_x
                out = out + coef[t, 1, at(c), :] * got_y
                out = out + coef[t, 2, at(c), :] * got_z
                if t == 0:
                    basis[j + 1, at(c), :] = basis[j + 1, at(c), :] + out
                else:
                    part[at(c), :] = out
            return 0

        lax.fori_loop(0, steps, transport, 0)

        def gram_step(c, accs):
            return tuple(
                acc + fold(ql[i, at(c), :] * pr[k, at(c), :])
                for (i, k), acc in zip(pairs(j), accs)
            )

        accs = lax.fori_loop(0, steps, gram_step, (zero,) * len(pairs(j)))
        gram = add_gram(gram, accs, j)

        for copy in passed:
            copy.wait_recv()

        def left_end(c, accs):
            total = ql[j + 1, at(c), :] + adjoint_part(far, 2, c) + adjoint_part(diagonal, 3, c)
            new = part[at(c), :] + freq * total
            ql[j + 1, at(c), :] = new
            return tuple(
                acc + fold(new * (ql[i, at(c), :] if i <= j else new))
                for i, acc in enumerate(accs)
            )

        left_dots = lax.fori_loop(0, steps, left_end, (zero,) * (j + 2))

        def right_end(c, accs):
            new = pr[j + 1, at(c), :] + freq * rs_xgot[at(c), :].astype(F32)
            pr[j + 1, at(c), :] = new
            return tuple(
                acc + fold(new * (pr[i, at(c), :] if i <= j else new))
                for i, acc in enumerate(accs)
            )

        right_dots = (zero,) * (j + 2)
        for h in range(2):
            shipped[h].wait_recv()
            right_dots = lax.fori_loop(
                h * (steps // 2), (h + 1) * (steps // 2), right_end, right_dots
            )
        for copy in across + [beside] + summed + shipped + passed:
            copy.wait_send()
        halo_sends("sent")

        sums = all_sum(to_tile(list(right_dots) + list(left_dots)), j + 1)
        right_coef = [pick(sums, i) for i in range(j + 1)]
        left_coef = [pick(sums, j + 2 + i) for i in range(j + 1)]
        right_raw, left_raw = pick(sums, j + 1), pick(sums, 2 * j + 3)
        for i in range(j + 1):
            right_raw = right_raw - right_coef[i] * right_coef[i]
            left_raw = left_raw - left_coef[i] * left_coef[i]
        right_norm = jnp.sqrt(right_raw + EPSILON)
        left_norm = jnp.sqrt(left_raw + EPSILON)
        for i in range(j + 2):
            here = (line == i) & (lane == j)
            right_hess = jnp.where(here, right_coef[i] if i <= j else right_norm, right_hess)
            left_hess = jnp.where(here, left_coef[i] if i <= j else left_norm, left_hess)
        inv_r, inv_l = 1.0 / right_norm, 1.0 / left_norm
        last = j == ITERS - 1

        def finish(c, accs):
            r, l = pr[j + 1, at(c), :], ql[j + 1, at(c), :]
            for i in range(j + 1):
                r = r - right_coef[i] * pr[i, at(c), :]
                l = l - left_coef[i] * ql[i, at(c), :]
            r, l = r * inv_r, l * inv_l
            pr[j + 1, at(c), :] = r
            ql[j + 1, at(c), :] = l
            if not last:
                wr[at(c), :] = r.astype(BF16)
                wl[0, at(c), :] = l.astype(BF16)
            return accs

        lax.fori_loop(0, steps, finish, 0)
        outgoing += leave(j + 1)

    def gram_last(c, accs):
        return tuple(
            acc + fold(ql[i, at(c), :] * pr[k, at(c), :])
            for (i, k), acc in zip(pairs(ITERS), accs)
        )

    accs = lax.fori_loop(0, steps, gram_last, (zero,) * len(pairs(ITERS)))
    total = all_sum(add_gram(gram, accs, ITERS), ITERS + 1)
    gram_tile = jnp.zeros((8, LANES), F32)
    for i in range(ITERS + 1):
        for k in range(ITERS + 1):
            gram_tile = jnp.where(
                (line == i) & (lane == k), pick(total, i * (ITERS + 1) + k), gram_tile
            )
    gram_out[...] = gram_tile[: ITERS + 1, : ITERS + 1]
    rh_out[...] = right_hess[: ITERS + 1, :ITERS]
    lh_out[...] = left_hess[: ITERS + 1, :ITERS]
    for copy in outgoing:
        copy.wait()


def per_device(
    start_right, start_left, collision, frequency, volume, face_neighbor, face_area, send_slot
):
    rows, cells = start_right.shape
    face = send_slot.shape[1]
    n_space, n_vel = lax.axis_size("space"), lax.axis_size("vel")
    assert n_vel == 4 and rows % (2 * CHUNK) == 0
    depth = cells + 4 * face
    tall = 2 * rows + 16
    vmem = pl.BlockSpec(memory_space=pltpu.VMEM)
    hbm = pl.BlockSpec(memory_space=pl.ANY)
    basis = jax.ShapeDtypeStruct((ITERS + 1, rows, cells), F32)
    hess = jax.ShapeDtypeStruct((ITERS + 1, ITERS), F32)
    dma = pltpu.SemaphoreType.DMA
    return pl.pallas_call(
        functools.partial(kernel, (n_space, n_vel, n_space // 4)),
        out_shape=(
            basis, basis, hess, hess, jax.ShapeDtypeStruct((ITERS + 1, ITERS + 1), F32)
        ),
        in_specs=[hbm] * 3 + [vmem] * 5,
        out_specs=(hbm, hbm, vmem, vmem, vmem),
        scratch_shapes=[
            pltpu.VMEM(collision.shape, BF16),
            pltpu.VMEM((collision.shape[1], rows), BF16),
            pltpu.VMEM((ITERS + 1, rows, cells), F32),
            pltpu.VMEM((ITERS + 1, rows, cells), F32),
            pltpu.VMEM((rows, cells), BF16),
            pltpu.VMEM((4, rows, cells), BF16),
            pltpu.VMEM((4, tall, face), BF16),
            pltpu.VMEM((4, tall, face), BF16),
            pltpu.VMEM((cells, 4 * face), BF16),
            pltpu.VMEM((depth, 6 * cells), BF16),
            pltpu.VMEM((16, cells), BF16),
            pltpu.VMEM((8, cells), F32),
            pltpu.VMEM((rows, cells), F32),
            pltpu.VMEM((2, 3, rows, cells), F32),
            pltpu.VMEM((rows, cells), F32),
            pltpu.VMEM((2, rows, cells), BF16),
            pltpu.VMEM((2, rows, cells), BF16),
            pltpu.VMEM((rows, cells), BF16),
            pltpu.VMEM((rows, cells), BF16),
            pltpu.VMEM((2, 8, LANES), F32),
            pltpu.VMEM((2, n_vel, 8, LANES), F32),
            pltpu.VMEM((2, 8, LANES), F32),
            pltpu.VMEM((2, n_space, 8, LANES), F32),
            dma((3,)),
            dma((2, ITERS + 1)),
            dma((5,)),
            dma((5,)),
            dma((4,)),
            dma((4,)),
            dma((4,)),
            dma((4,)),
            dma((2, n_vel)),
            dma((2, n_vel)),
            dma((2, n_space)),
            dma((2, n_space)),
        ],
        compiler_params=pltpu.CompilerParams(
            collective_id=0, has_side_effects=True, vmem_limit_bytes=60 * 1024 * 1024
        ),
    )(
        start_right, start_left, collision, frequency.reshape(1, -1), volume.reshape(1, -1),
        face_neighbor, face_area, send_slot.reshape(1, -1),
    )


def solution(mesh):
    placed = (
        P("vel", "space"),
        P("vel", "space"),
        P("vel", None),
        P("space"),
        P("space"),
        P(None, "space"),
        P(None, "space"),
        P(None, "space"),
    )
    return jax.shard_map(
        per_device,
        mesh=mesh,
        in_specs=placed,
        out_specs=(P(None, "vel", "space"), P(None, "vel", "space"), P(), P(), P()),
        check_vma=False,
    )
```
